32 devices in a mesh: groups: 2 (over y), atoms: 4 (over z), chan: 2 (over x), sub: 2 (over core).
Axes of the slice: x: 2, y: 2, z: 4, core: 2. Of those that a mesh axis runs over, the one named last changes fastest.
Arguments:
- cotangent: bfloat16 [29, 64, 12288], P(None, ('chan', 'sub'), ('groups', 'atoms')), parts along dimension 2, may hold values from -6 to 6
- wigner: bfloat16 [235, 12288], P(None, ('groups', 'atoms')), parts along dimension 1, may hold values from -2.390625 to 2.390625
- sender_ids: int32 [12288], P(('groups', 'atoms')), parts along dimension 0, may hold values from 0 to 63, as said below
- receiver_slots: int32 [12288], P(('groups', 'atoms')), parts along dimension 0, may hold values from 0 to 31
- destinations: int32 [96], P(('groups', 'atoms')), parts along dimension 0, may hold values from 0 to 3, as said below
- live_counts: int32 [96], P(('groups', 'atoms')), parts along dimension 0, may hold values from 32 to 128, as said below
- receiver_lists: int32 [96, 32], P(('groups', 'atoms')), parts along dimension 0, may hold values from 0 to 63, as said below
- weight_zero: bfloat16 [7, 2, 128, 7, 64], P(None, None, ('chan', 'sub')), may hold values from -0.125 to 0.125
- real_one: bfloat16 [6, 2, 128, 6, 64], P(None, None, ('chan', 'sub')), may hold values from -0.15625 to 0.15625
- imag_one: bfloat16 [6, 2, 128, 6, 64], P(None, None, ('chan', 'sub')), may hold values from -0.15625 to 0.15625
- real_two: bfloat16 [5, 2, 128, 5, 64], P(None, None, ('chan', 'sub')), may hold values from -0.15625 to 0.15625
- imag_two: bfloat16 [5, 2, 128, 5, 64], P(None, None, ('chan', 'sub')), may hold values from -0.15625 to 0.15625
- to_grid: bfloat16 [196, 49], replicated, may hold values from -0.875 to 0.875
- from_grid: bfloat16 [49, 196], replicated, may hold values from -0.4375 to 0.4375
- pre_act: bfloat16 [49, 128, 512], P(None, ('chan', 'sub'), ('groups', 'atoms')), parts along dimension 2, may hold values from -6 to 6
Outputs:
- grad_pre: bfloat16 [49, 128, 512], P(None, ('chan', 'sub'), ('groups', 'atoms')), parts along dimension 2
The draws below stay inside these ranges and needn't reach their ends.
There are 2 independent parts, one for each index of `groups`. The reference program is written for one: setup_inputs(seed, part) draws one part's arguments, and reference() takes and returns one part's arrays. A program takes and returns all parts, laid end to end along the dimension named above; an argument that names none is the same for every part. Nothing has to cross between parts.
Inputs may be any that keep to these rules, and one draw needn't show every extreme that they name: `sender_ids`: within one shard's edges the senders never fall. `destinations`: the blocks of one shard name each shard at most 3 times, and some shard exactly that often. `live_counts`: live edges stand at the head of a block; the rest is padding. Some block of every shard is full. `receiver_lists`: each block lists 32 distinct atoms of its destination shard.
All inputs are finite; a program needn't handle non-finite values.
Results may differ from the reference program's by a relative error of at most 0.0068.
Values may be sent and summed in bfloat16 or wider, within the bound.
A program may use at most 128 MiB of HBM per device.

```python
import jax
import jax.numpy as jnp
from jax import lax

C = 128
COUT = 64
COEF = 49
EDGE_COEF = 29
WIGNER_ROWS = 235
G = 196
EDGE_BLOCK = 128
ATOM_DEV = 64
BLOCKS = 12
RECV_SLOTS = 32
SLOTS_PER_DEST = 3
ATOMS = 256
EDGES = 6144
N_ATOMS = 4


def draw_sender_ids(key, part):
    key = jax.random.fold_in(key, 11)
    raw_ids = jax.random.randint(key, (N_ATOMS, BLOCKS * EDGE_BLOCK), 0, ATOM_DEV)
    raw_ids = raw_ids.at[:, 0].set(0).at[:, -1].set(ATOM_DEV - 1)
    return jnp.sort(raw_ids, axis=1).reshape(-1).astype(jnp.int32)


def draw_receiver_slots(key, part):
    key = jax.random.fold_in(key, 12)
    raw_slots = jax.random.randint(key, (N_ATOMS * BLOCKS * EDGE_BLOCK,), 0, RECV_SLOTS)
    return raw_slots.at[0].set(0).at[1].set(RECV_SLOTS - 1).astype(jnp.int32)


def draw_destinations(key, part):
    key = jax.random.fold_in(key, 13)
    shard_keys = jax.random.split(key, N_ATOMS)
    repeated = jnp.tile(jnp.arange(N_ATOMS, dtype=jnp.int32), SLOTS_PER_DEST)

    def one_shard(shard_key):
        return jax.random.permutation(shard_key, repeated)[:BLOCKS]
    return jax.vmap(one_shard)(shard_keys).reshape(-1).astype(jnp.int32)


def draw_live_counts(key, part):
    key = jax.random.fold_in(key, 14)
    raw_counts = jax.random.randint(key, (N_ATOMS, BLOCKS), EDGE_BLOCK // 4, EDGE_BLOCK + 1)
    return raw_counts.at[:, 0].set(EDGE_BLOCK).reshape(-1).astype(jnp.int32)


def draw_receiver_lists(key, part):
    key = jax.random.fold_in(key, 15)
    block_keys = jax.random.split(key, N_ATOMS * BLOCKS)

    def one_block(block_key):
        return jax.random.permutation(block_key, ATOM_DEV)[:RECV_SLOTS]
    return jax.vmap(one_block)(block_keys).astype(jnp.int32)


def level_of(own_key, shape, pieces, least, high):
    factor_of, own = 1.0, jax.random.fold_in(own_key, 6)
    for axis_at, parts in pieces:
        heights = jnp.exp(jax.random.uniform(jax.random.fold_in(own, axis_at), (parts,), jnp.float32, least / len(pieces), high / len(pieces)))
        factor_of = factor_of * jnp.repeat(heights, shape[axis_at] // parts).reshape([-1 if axis == axis_at else 1 for axis in range(len(shape))])
    return factor_of


def noise(key, shape, spread, reach, cuts=(), kind=jnp.bfloat16):
    values = spread * jax.random.normal(key, shape, jnp.float32)
    if cuts:
        values = values * level_of(key, shape, cuts, -0.22, 0.18)
    return jnp.clip(values, -reach, reach).astype(kind)


def setup_inputs(seed: int = 0, part: int = 0) -> dict:
    key_list = jax.random.split(jax.random.key(seed), 16)
    part_keys = jax.random.split(jax.random.fold_in(key_list[15], part), 16)
    cotangent = noise(part_keys[0], (EDGE_COEF, COUT, EDGES), 1.0, 6.0, ((1, 4), (2, 4)))
    wigner = noise(part_keys[1], (WIGNER_ROWS, EDGES), 0.4, 2.390625, ((1, 4),))
    sender_ids = draw_sender_ids(jax.random.fold_in(jax.random.fold_in(key_list[15], part), 71), part)
    receiver_slots = draw_receiver_slots(jax.random.fold_in(jax.random.fold_in(key_list[15], part), 71), part)
    destinations = draw_destinations(jax.random.fold_in(jax.random.fold_in(key_list[15], part), 71), part)
    live_counts = draw_live_counts(jax.random.fold_in(jax.random.fold_in(key_list[15], part), 71), part)
    receiver_lists = draw_receiver_lists(jax.random.fold_in(jax.random.fold_in(key_list[15], part), 71), part)
    weight_zero = noise(key_list[7], (7, 2, C, 7, COUT), (14 * C) ** -0.5, 0.125, ((2, 4),))
    real_one = noise(key_list[8], (6, 2, C, 6, COUT), (12 * C) ** -0.5, 0.15625, ((2, 4),))
    imag_one = noise(key_list[9], (6, 2, C, 6, COUT), (12 * C) ** -0.5, 0.15625, ((2, 4),))
    real_two = noise(key_list[10], (5, 2, C, 5, COUT), (10 * C) ** -0.5, 0.15625, ((2, 4),))
    imag_two = noise(key_list[11], (5, 2, C, 5, COUT), (10 * C) ** -0.5, 0.15625, ((2, 4),))
    to_grid = noise(key_list[12], (G, COEF), COEF ** -0.5, 0.875)
    from_grid = noise(key_list[13], (COEF, G), G ** -0.5, 0.4375)
    pre_act = noise(part_keys[14], (COEF, C, ATOMS), 1.0, 6.0, ((1, 4), (2, 4)))
    return dict(cotangent=cotangent, wigner=wigner, sender_ids=sender_ids, receiver_slots=receiver_slots, destinations=destinations, live_counts=live_counts, receiver_lists=receiver_lists, weight_zero=weight_zero, real_one=real_one, imag_one=imag_one, real_two=real_two, imag_two=imag_two, to_grid=to_grid, from_grid=from_grid, pre_act=pre_act)


def contract(weight, piece):
    return jnp.einsum("ahcbq,bqe->ahce", weight, piece, preferred_element_type=jnp.float32)


def so2_transpose(piece, weights):
    weight_zero, real_one, imag_one, real_two, imag_two = weights
    zero_rows = contract(weight_zero, piece[0:7])
    plus_one = contract(real_one, piece[7:13]) + contract(imag_one, piece[13:19])
    minus_one = contract(real_one, piece[13:19]) - contract(imag_one, piece[7:13])
    plus_two = contract(real_two, piece[19:24]) + contract(imag_two, piece[24:29])
    minus_two = contract(real_two, piece[24:29]) - contract(imag_two, piece[19:24])
    return (zero_rows, plus_one, minus_one, plus_two, minus_two)


def rotate_back(grad_parts, wigner):
    zero_rows, plus_one, minus_one, plus_two, minus_two = grad_parts
    pieces_out = []
    offset = 0
    for degree in range(7):
        m_reach = min(degree, 2)
        edge_rows = []
        if m_reach >= 2:
            edge_rows.append(minus_two[degree - 2])
        if m_reach >= 1:
            edge_rows.append(minus_one[degree - 1])
        edge_rows.append(zero_rows[degree])
        if m_reach >= 1:
            edge_rows.append(plus_one[degree - 1])
        if m_reach >= 2:
            edge_rows.append(plus_two[degree - 2])
        span_width = 2 * degree + 1
        summed = jnp.zeros((span_width,) + edge_rows[0].shape, jnp.float32)
        for position, edge_row in enumerate(edge_rows):
            start_row = offset + position * span_width
            coeffs = wigner[start_row:start_row + span_width].astype(jnp.float32)
            summed = summed + coeffs[:, None, None, :] * edge_row[None]
        offset = offset + len(edge_rows) * span_width
        pieces_out.append(summed.astype(jnp.bfloat16))
    return jnp.concatenate(pieces_out, axis=0)


def sphere_backward(to_grid, from_grid, pre_flat, atom_grad):
    grid_pre = jnp.dot(to_grid, pre_flat, preferred_element_type=jnp.float32)
    grid_grad = lax.dot_general(from_grid, atom_grad, (((0,), (0,)), ((), ())), preferred_element_type=jnp.float32)
    sigmoid_of = jax.nn.sigmoid(grid_pre)
    grid_term = (sigmoid_of * (1.0 + grid_pre * (1.0 - sigmoid_of)) * grid_grad).astype(jnp.bfloat16)
    return lax.dot_general(to_grid, grid_term, (((0,), (0,)), ((), ())), preferred_element_type=jnp.float32).astype(jnp.bfloat16)


def reference(cotangent, wigner, sender_ids, receiver_slots, destinations, live_counts, receiver_lists, weight_zero, real_one, imag_one, real_two, imag_two, to_grid, from_grid, pre_act):
    shard_edges = BLOCKS * EDGE_BLOCK
    weights = (weight_zero, real_one, imag_one, real_two, imag_two)
    cot_shards = cotangent.reshape(EDGE_COEF, COUT, N_ATOMS, shard_edges).transpose(2, 0, 1, 3)
    wig_shards = wigner.reshape(WIGNER_ROWS, N_ATOMS, shard_edges).transpose(1, 0, 2)
    send_shards = sender_ids.reshape(N_ATOMS, shard_edges)
    slot_shards = receiver_slots.reshape(N_ATOMS, shard_edges)
    count_shards = live_counts.reshape(N_ATOMS, BLOCKS)

    def per_shard(shard_items):
        cot_one, wig_one, send_one, slot_one, count_one = shard_items
        rotated = rotate_back(so2_transpose(cot_one, weights), wig_one)
        position = jnp.arange(shard_edges, dtype=jnp.int32)
        block_of = position // EDGE_BLOCK
        live_edge = (position % EDGE_BLOCK) < jnp.repeat(count_one, EDGE_BLOCK)
        sender_rows = rotated[:, 0].reshape(COEF * C, shard_edges).T.astype(jnp.float32)
        sender_index = jnp.where(live_edge, send_one, ATOM_DEV).astype(jnp.int32)
        sender_sum = jax.ops.segment_sum(sender_rows, sender_index, num_segments=ATOM_DEV + 1)[:ATOM_DEV]
        receiver_rows = rotated[:, 1].reshape(COEF * C, shard_edges).T.astype(jnp.float32)
        slot_index = jnp.where(live_edge, block_of * RECV_SLOTS + slot_one, BLOCKS * RECV_SLOTS).astype(jnp.int32)
        block_sum = jax.ops.segment_sum(receiver_rows, slot_index, num_segments=BLOCKS * RECV_SLOTS + 1)[:BLOCKS * RECV_SLOTS]
        return sender_sum, block_sum.astype(jnp.bfloat16)

    sender_all, block_all = lax.map(per_shard, (cot_shards, wig_shards, send_shards, slot_shards, count_shards))
    atom_ids = (destinations[:, None] * ATOM_DEV + receiver_lists).reshape(-1).astype(jnp.int32)
    receiver_sum = jax.ops.segment_sum(block_all.reshape(-1, COEF * C).astype(jnp.float32), atom_ids, num_segments=ATOMS)
    atom_grad = (sender_all.reshape(ATOMS, COEF * C) + receiver_sum).astype(jnp.bfloat16)
    atom_grad = atom_grad.reshape(ATOMS, COEF, C).transpose(1, 2, 0).reshape(COEF, C * ATOMS)
    result = sphere_backward(to_grid, from_grid, pre_act.reshape(COEF, C * ATOMS), atom_grad)
    return result.reshape(COEF, C, ATOMS)
```

```python
import functools

import jax
import jax.numpy as jnp
from jax import lax
from jax.experimental import pallas as pl
from jax.experimental.pallas import tpu as pltpu
from jax.sharding import PartitionSpec as P


def contract(weight, piece):
    return jnp.einsum("ahcbq,bqe->ahce", weight, piece, preferred_element_type=jnp.float32)


def so2_transpose(piece, weights):
    weight_zero, real_one, imag_one, real_two, imag_two = weights
    zero_rows = contract(weight_zero, piece[0:7])
    plus_one = contract(real_one, piece[7:13]) + contract(imag_one, piece[13:19])
    minus_one = contract(real_one, piece[13:19]) - contract(imag_one, piece[7:13])
    plus_two = contract(real_two, piece[19:24]) + contract(imag_two, piece[24:29])
    minus_two = contract(real_two, piece[24:29]) - contract(imag_two, piece[19:24])
    return (zero_rows, plus_one, minus_one, plus_two, minus_two)


def rotate_back(grad_parts, wigner):
    zero_rows, plus_one, minus_one, plus_two, minus_two = grad_parts
    pieces_out = []
    offset = 0
    for degree in range(7):
        m_reach = min(degree, 2)
        edge_rows = []
        if m_reach >= 2:
            edge_rows.append(minus_two[degree - 2])
        if m_reach >= 1:
            edge_rows.append(minus_one[degree - 1])
        edge_rows.append(zero_rows[degree])
        if m_reach >= 1:
            edge_rows.append(plus_one[degree - 1])
        if m_reach >= 2:
            edge_rows.append(plus_two[degree - 2])
        span_width = 2 * degree + 1
        summed = jnp.zeros((span_width,) + edge_rows[0].shape, jnp.float32)
        for position, edge_row in enumerate(edge_rows):
            start_row = offset + position * span_width
            coeffs = wigner[start_row : start_row + span_width].astype(jnp.float32)
            summed = summed + coeffs[:, None, None, :] * edge_row[None]
        offset = offset + len(edge_rows) * span_width
        pieces_out.append(summed.astype(jnp.bfloat16))
    return jnp.concatenate(pieces_out, axis=0)


def sphere_backward(to_grid, from_grid, pre_flat, atom_grad):
    grid_pre = jnp.dot(to_grid, pre_flat, preferred_element_type=jnp.float32)
    grid_grad = lax.dot_general(
        from_grid, atom_grad, (((0,), (0,)), ((), ())), preferred_element_type=jnp.float32
    )
    sigmoid_of = jax.nn.sigmoid(grid_pre)
    grid_term = (sigmoid_of * (1.0 + grid_pre * (1.0 - sigmoid_of)) * grid_grad).astype(
        jnp.bfloat16
    )
    return lax.dot_general(
        to_grid, grid_term, (((0,), (0,)), ((), ())), preferred_element_type=jnp.float32
    ).astype(jnp.bfloat16)


def add_parts(right_parts):
    return tuple((right_one for right_one in right_parts))


def per_device_general(
    cotangent,
    wigner,
    sender_ids,
    receiver_slots,
    destinations,
    live_counts,
    receiver_lists,
    weight_zero,
    real_one,
    imag_one,
    real_two,
    imag_two,
    to_grid,
    from_grid,
    pre_act,
):
    edge_total = cotangent.shape[2]
    block_count = destinations.shape[0]
    block_width = edge_total // block_count
    coef_rows = pre_act.shape[0]
    chan_share = pre_act.shape[1]
    atom_share = pre_act.shape[2]
    slot_width = receiver_lists.shape[1]
    shard_count = lax.axis_size("atoms")
    per_dest = (block_count + shard_count - 1) // shard_count
    slot_total = shard_count * per_dest
    weights = (weight_zero, real_one, imag_one, real_two, imag_two)
    weight_cols = tuple((weight for weight in weights))
    grad_parts = add_parts(
        so2_transpose(lax.all_gather(cotangent, ("chan", "sub"), axis=1, tiled=True), weight_cols)
    )
    rotated = rotate_back(grad_parts, wigner)
    live_edge = (
        lax.broadcasted_iota(jnp.int32, (block_count, block_width), 1) < live_counts[:, None]
    )
    live_flat = live_edge.reshape(edge_total)
    atom_axis = jnp.arange(atom_share, dtype=jnp.int32)
    sender_rows = rotated[:, 0].reshape(coef_rows * chan_share, edge_total)
    sender_hot = ((sender_ids[:, None] == atom_axis[None, :]) & live_flat[:, None]).astype(
        jnp.bfloat16
    )
    sender_sum = jnp.dot(sender_rows, sender_hot, preferred_element_type=jnp.float32)
    receiver_rows = rotated[:, 1].reshape(coef_rows * chan_share, block_count, block_width)
    slot_grid = receiver_slots.reshape(block_count, block_width)
    slot_axis = jnp.arange(slot_width, dtype=jnp.int32)
    block_axis = jnp.arange(block_count, dtype=jnp.int32)
    same_dest = destinations[:, None] == destinations[None, :]
    earlier = jnp.sum(same_dest & (block_axis[:, None] > block_axis[None, :]), axis=1)
    placement = destinations * per_dest + earlier
    place_hot = placement[:, None] == jnp.arange(slot_total, dtype=jnp.int32)[None, :]
    slot_hot = ((slot_grid[:, :, None] == slot_axis[None, None, :]) & live_edge[:, :, None]).astype(
        jnp.bfloat16
    )
    block_sums = jnp.einsum(
        "kbw,bwr->bkr", receiver_rows, slot_hot, preferred_element_type=jnp.float32
    ).astype(jnp.bfloat16)
    send_sums = jnp.einsum(
        "bs,bkr->ksr",
        place_hot.astype(jnp.bfloat16),
        block_sums,
        preferred_element_type=jnp.float32,
    ).astype(jnp.bfloat16)
    list_send = (
        jnp.sum(place_hot.astype(jnp.int32)[:, :, None] * (receiver_lists[:, None, :] + 1), axis=0)
        - 1
    )
    list_wire = list_send.astype(jnp.float32).astype(jnp.bfloat16)[None]
    got_sums, got_lists = (
        lax.all_to_all(send_sums, "atoms", split_axis=1, concat_axis=1, tiled=True),
        lax.all_to_all(list_wire, "atoms", split_axis=1, concat_axis=1, tiled=True),
    )
    got_ids = got_lists[0].astype(jnp.float32).astype(jnp.int32).reshape(slot_total * slot_width)
    got_hot = (got_ids[:, None] == atom_axis[None, :]).astype(jnp.bfloat16)
    receiver_sum = jnp.dot(
        got_sums.reshape(coef_rows * chan_share, slot_total * slot_width),
        got_hot,
        preferred_element_type=jnp.float32,
    )
    atom_grad = (
        (sender_sum + receiver_sum).astype(jnp.bfloat16).reshape(coef_rows, chan_share * atom_share)
    )
    result = sphere_backward(
        to_grid, from_grid, pre_act.reshape(coef_rows, chan_share * atom_share), atom_grad
    )
    return result.reshape(coef_rows, chan_share, atom_share)


MESH = pl.DeviceIdType.MESH
F32 = jnp.float32
BF16 = jnp.bfloat16


def dot_last(left, right):
    return lax.dot_general(left, right, (((1,), (1,)), ((), ())), preferred_element_type=F32)


def dot_first(left, right):
    return lax.dot_general(left, right, (((0,), (0,)), ((), ())), preferred_element_type=F32)


def rotate_chunk(grads, wig, rotated, columns):
    offset = 0
    for degree in range(7):
        reach = min(degree, 2)
        starts = {-2: 22 + degree, -1: 12 + degree, 0: degree, 1: 6 + degree, 2: 17 + degree}
        rows = [grads[pl.ds(64 * starts[m], 64), columns] for m in range(-reach, reach + 1)]
        width = 2 * degree + 1
        for p in range(width):
            total = None
            for position, row in enumerate(rows):
                at = offset + position * width + p
                term = wig[at : at + 1, columns] * row
                total = term if total is None else total + term
            total = total.astype(BF16)
            for half in range(4):
                rotated[
                    half // 2, half % 2, degree * degree + p, :, columns
                ] = total[16 * half : 16 * half + 16]
        offset += len(rows) * width


def fused_kernel(
    chunks,
    cot,
    wigner,
    senders,
    slots,
    dests,
    lives,
    lists,
    wzero,
    wone,
    wtwo,
    to_grid,
    from_grid,
    pre,
    out,
    gathered,
    grads,
    wig,
    rotated,
    hot_recv,
    hot_send,
    acc_recv,
    acc_send,
    send_to,
    recv_to,
    message,
    arrived,
    slope,
    packed,
    tall,
    flat,
    local_sem,
    out_sem,
    in_sem,
    far_out,
    far_in,
):
    x = lax.axis_index("chan")
    core = lax.axis_index("sub")
    z = lax.axis_index("atoms")
    shards = message.shape[0]
    atoms = acc_send.shape[1]
    me, xpart = 2 * x + core, 2 * (1 - x) + core
    cpart, dpart = 2 * x + 1 - core, 2 * (1 - x) + 1 - core
    to_core, to_chip = {"sub": 1 - core}, {"chan": 1 - x}
    edges = cot.shape[2]
    wide = edges // chunks

    barrier = pltpu.get_barrier_semaphore()
    pl.semaphore_signal(barrier, inc=1, device_id=to_core, device_id_type=MESH)
    pl.semaphore_signal(barrier, inc=1, device_id=to_chip, device_id_type=MESH)
    for step in range(1, shards):
        pl.semaphore_signal(
            barrier, inc=1, device_id={"atoms": lax.rem(z + step, shards)}, device_id_type=MESH
        )
    pl.semaphore_wait(barrier, shards + 1)

    def span(j):
        return pl.ds(pl.multiple_of(j * wide, wide), wide)

    def own_copy(j, kind, target):
        return pltpu.make_async_remote_copy(
            src_ref=cot.at[:, :, span(j)],
            dst_ref=gathered.at[:, me, :, span(j)],
            send_sem=out_sem.at[kind, j],
            recv_sem=in_sem.at[kind, j],
            device_id=target,
            device_id_type=MESH,
        )

    def arrival(j, kind, origin, target):
        return pltpu.make_async_remote_copy(
            src_ref=gathered.at[:, origin, :, span(j)],
            dst_ref=gathered.at[:, origin, :, span(j)],
            send_sem=out_sem.at[kind, j],
            recv_sem=in_sem.at[kind, j],
            device_id=target,
            device_id_type=MESH,
        )

    def start_chunk(j, carry):
        own_copy(j, 1, to_chip).start()
        own_copy(j, 0, to_core).start()
        return carry

    lax.fori_loop(0, chunks, start_chunk, 0)
    keep = pltpu.make_async_copy(cot, gathered.at[:, me], local_sem)
    keep.start()

    blocks, block = slots.shape
    live = lax.broadcasted_iota(jnp.int32, (blocks, block), 1) < lives[...]
    listed = jnp.zeros((blocks, block), jnp.int32)
    for slot in range(lists.shape[1]):
        listed = jnp.where(slots[...] == slot, lists[:, slot : slot + 1], listed)
    recv_to[...] = jnp.where(live, dests[...] * atoms + listed, -1)
    send_to[...] = jnp.where(live, senders[...], -1)
    acc_recv[...] = jnp.zeros_like(acc_recv)
    acc_send[...] = jnp.zeros_like(acc_send)

    packed[:, 0:atoms] = pre[...].astype(F32)
    packed[:, atoms:128] = jnp.zeros((packed.shape[0], 128 - atoms), F32)
    coefs = to_grid.shape[1]
    for c in range(16):
        pair = [
            packed[pl.ds(16 * half + c, coefs, stride=32), :][:, 0:atoms] for half in range(2)
        ]
        flat[:, 128 * c : 128 * c + 128] = jnp.concatenate(pair, axis=1).astype(BF16)

    def slope_part(i, carry):
        columns = pl.ds(pl.multiple_of(i * 256, 256), 256)
        value = jnp.dot(to_grid[...], flat[:, columns], preferred_element_type=F32)
        sig = 1.0 / (1.0 + jnp.exp(-value))
        slope[:, columns] = sig * (1.0 + value * (1.0 - sig))
        return carry

    lax.fori_loop(0, 8, slope_part, 0)
    keep.wait()

    def work(j, carry):
        arrival(j, 1, xpart, to_chip).wait_recv()
        arrival(j, 2, xpart, to_core).start()
        arrival(j, 0, cpart, to_core).wait_recv()
        arrival(j, 2, dpart, to_core).wait_recv()
        piece = gathered[:, :, :, span(j)].reshape(29 * 64, wide)
        grads[0:448] = jnp.dot(wzero[...], piece[0:448], preferred_element_type=F32)
        grads[448:1216] = jnp.dot(wone[...], piece[448:1216], preferred_element_type=F32)
        grads[1216:1856] = jnp.dot(wtwo[...], piece[1216:1856], preferred_element_type=F32)
        wig[...] = wigner[:, span(j)].astype(F32)

        for i in range(wide // block):
            columns = pl.ds(i * block, block)
            rotate_chunk(grads, wig, rotated, columns)
            row = pl.ds(j * (wide // block) + i, 1)
            hot_recv[:, columns] = (
                lax.broadcasted_iota(jnp.int32, (hot_recv.shape[0], block), 0) == recv_to[row, :]
            ).astype(F32).astype(BF16)
            hot_send[:, columns] = (
                lax.broadcasted_iota(jnp.int32, (hot_send.shape[0], block), 0) == send_to[row, :]
            ).astype(F32).astype(BF16)
        height = acc_recv.shape[0]
        acc_recv[...] += dot_last(rotated[1].reshape(height, wide), hot_recv[...])
        acc_send[...] += dot_last(rotated[0].reshape(height, wide), hot_send[...])
        return carry

    lax.fori_loop(0, chunks, work, 0)

    half_rows = acc_recv.shape[0] // 2
    for d in range(shards):
        cut = slice(atoms * d, atoms * d + atoms)
        message[d] = jnp.concatenate(
            [acc_recv[0:half_rows, cut], acc_recv[half_rows:, cut]], axis=1
        ).astype(BF16)

    def far_copy(step):
        return pltpu.make_async_remote_copy(
            src_ref=message.at[lax.rem(z + step, shards)],
            dst_ref=arrived.at[step - 1],
            send_sem=far_out.at[step - 1],
            recv_sem=far_in.at[step - 1],
            device_id={"atoms": lax.rem(z + step, shards)},
            device_id_type=MESH,
        )

    for step in range(1, shards):
        far_copy(step).start()
    total = jnp.concatenate([acc_send[0:half_rows], acc_send[half_rows:]], axis=1)
    total = total + message[z].astype(F32)
    for step in range(1, shards):
        far_copy(step).wait_recv()
        total = total + arrived[step - 1].astype(F32)
    tall[...] = total
    for c in range(16):
        flat[:, 128 * c : 128 * c + 128] = tall[pl.ds(c, coefs, stride=16), :].astype(BF16)
    for i in range(8):
        columns = slice(256 * i, 256 * i + 256)
        term = (slope[:, columns] * dot_first(from_grid[...], flat[:, columns])).astype(BF16)
        result = dot_first(to_grid[...], term)
        for c in range(2):
            tall[pl.ds(2 * i + c, coefs, stride=16), :] = result[:, 128 * c : 128 * c + 128]
    done = tall[...].astype(BF16).reshape(coefs, 16, 128)
    out[:, 0:16, :] = done[:, :, 0:atoms]
    out[:, 16:32, :] = done[:, :, atoms:128]

    def finish(j, carry):
        own_copy(j, 1, to_chip).wait_send()
        own_copy(j, 0, to_core).wait_send()
        arrival(j, 2, xpart, to_core).wait_send()
        return carry

    lax.fori_loop(0, chunks, finish, 0)
    for step in range(1, shards):
        far_copy(step).wait_send()


def per_device(
    mesh,
    cotangent,
    wigner,
    sender_ids,
    receiver_slots,
    destinations,
    live_counts,
    receiver_lists,
    weight_zero,
    real_one,
    imag_one,
    real_two,
    imag_two,
    to_grid,
    from_grid,
    pre_act,
):
    edges = cotangent.shape[2]
    blocks = destinations.shape[0]
    block = edges // blocks
    coefs, chan_share, atoms = pre_act.shape
    shards = mesh.shape["atoms"]
    fits = (
        mesh.shape["chan"] == 2
        and mesh.shape["sub"] == 2
        and cotangent.shape[1] == 16
        and chan_share == 32
        and atoms == 64
        and block == 128
        and blocks % 2 == 0
        and 1 < shards <= 4
    )
    if not fits:
        return per_device_general(
            cotangent,
            wigner,
            sender_ids,
            receiver_slots,
            destinations,
            live_counts,
            receiver_lists,
            weight_zero,
            real_one,
            imag_one,
            real_two,
            imag_two,
            to_grid,
            from_grid,
            pre_act,
        )

    def paired(real, imag):
        size = real.shape[0] * 64
        real, imag = real.reshape(size, size), imag.reshape(size, size)
        return jnp.concatenate(
            [jnp.concatenate([real, imag], axis=1), jnp.concatenate([-imag, real], axis=1)], axis=0
        )

    chunks = blocks // 2
    wide = 2 * block
    height = coefs * chan_share
    points = to_grid.shape[0]
    vmem = pl.BlockSpec(memory_space=pltpu.VMEM)
    return pl.pallas_call(
        functools.partial(fused_kernel, chunks),
        out_shape=jax.ShapeDtypeStruct(pre_act.shape, BF16),
        in_specs=[vmem] * 13,
        out_specs=vmem,
        scratch_shapes=[
            pltpu.VMEM((29, 4, 16, edges), BF16),
            pltpu.VMEM((29 * 64, wide), F32),
            pltpu.VMEM((wigner.shape[0], wide), F32),
            pltpu.VMEM((2, 2, coefs, 16, wide), BF16),
            pltpu.VMEM((shards * atoms, wide), BF16),
            pltpu.VMEM((atoms, wide), BF16),
            pltpu.VMEM((height, shards * atoms), F32),
            pltpu.VMEM((height, atoms), F32),
            pltpu.VMEM((blocks, block), jnp.int32),
            pltpu.VMEM((blocks, block), jnp.int32),
            pltpu.VMEM((shards, height // 2, 2 * atoms), BF16),
            pltpu.VMEM((shards - 1, height // 2, 2 * atoms), BF16),
            pltpu.VMEM((points, chan_share * atoms), F32),
            pltpu.VMEM((height, 128), F32),
            pltpu.VMEM((height // 2, 128), F32),
            pltpu.VMEM((coefs, chan_share * atoms), BF16),
            pltpu.SemaphoreType.DMA,
            pltpu.SemaphoreType.DMA((3, chunks)),
            pltpu.SemaphoreType.DMA((3, chunks)),
            pltpu.SemaphoreType.DMA((shards - 1,)),
            pltpu.SemaphoreType.DMA((shards - 1,)),
        ],
        compiler_params=pltpu.CompilerParams(
            collective_id=0, has_side_effects=True, vmem_limit_bytes=50 * 2**20
        ),
    )(
        cotangent,
        wigner,
        sender_ids.reshape(blocks, block),
        receiver_slots.reshape(blocks, block),
        destinations.reshape(blocks, 1),
        live_counts.reshape(blocks, 1),
        receiver_lists,
        weight_zero.reshape(448, 448),
        paired(real_one, imag_one),
        paired(real_two, imag_two),
        to_grid,
        from_grid,
        pre_act.reshape(height, atoms),
    )


def solution(mesh):
    in_specs = (
        P(None, ("chan", "sub"), ("groups", "atoms")),
        P(None, ("groups", "atoms")),
        P(("groups", "atoms")),
        P(("groups", "atoms")),
        P(("groups", "atoms")),
        P(("groups", "atoms")),
        P(("groups", "atoms"), None),
        P(None, None, ("chan", "sub"), None, None),
        P(None, None, ("chan", "sub"), None, None),
        P(None, None, ("chan", "sub"), None, None),
        P(None, None, ("chan", "sub"), None, None),
        P(None, None, ("chan", "sub"), None, None),
        P(),
        P(),
        P(None, ("chan", "sub"), ("groups", "atoms")),
    )
    out_specs = P(None, ("chan", "sub"), ("groups", "atoms"))
    return jax.shard_map(
        functools.partial(per_device, mesh), mesh=mesh, in_specs=in_specs, out_specs=out_specs, check_vma=False
    )
```

```python
import functools

import jax
import jax.numpy as jnp
from jax import lax
from jax.experimental import pallas as pl
from jax.experimental.pallas import tpu as pltpu
from jax.sharding import PartitionSpec as P


def contract(weight, piece):
    return jnp.einsum("ahcbq,bqe->ahce", weight, piece, preferred_element_type=jnp.float32)


def so2_transpose(piece, weights):
    weight_zero, real_one, imag_one, real_two, imag_two = weights
    zero_rows = contract(weight_zero, piece[0:7])
    plus_one = contract(real_one, piece[7:13]) + contract(imag_one, piece[13:19])
    minus_one = contract(real_one, piece[13:19]) - contract(imag_one, piece[7:13])
    plus_two = contract(real_two, piece[19:24]) + contract(imag_two, piece[24:29])
    minus_two = contract(real_two, piece[24:29]) - contract(imag_two, piece[19:24])
    return (zero_rows, plus_one, minus_one, plus_two, minus_two)


def rotate_back(grad_parts, wigner):
    zero_rows, plus_one, minus_one, plus_two, minus_two = grad_parts
    pieces_out = []
    offset = 0
    for degree in range(7):
        m_reach = min(degree, 2)
        edge_rows = []
        if m_reach >= 2:
            edge_rows.append(minus_two[degree - 2])
        if m_reach >= 1:
            edge_rows.append(minus_one[degree - 1])
        edge_rows.append(zero_rows[degree])
        if m_reach >= 1:
            edge_rows.append(plus_one[degree - 1])
        if m_reach >= 2:
            edge_rows.append(plus_two[degree - 2])
        span_width = 2 * degree + 1
        summed = jnp.zeros((span_width,) + edge_rows[0].shape, jnp.float32)
        for position, edge_row in enumerate(edge_rows):
            start_row = offset + position * span_width
            coeffs = wigner[start_row : start_row + span_width].astype(jnp.float32)
            summed = summed + coeffs[:, None, None, :] * edge_row[None]
        offset = offset + len(edge_rows) * span_width
        pieces_out.append(summed.astype(jnp.bfloat16))
    return jnp.concatenate(pieces_out, axis=0)


def sphere_backward(to_grid, from_grid, pre_flat, atom_grad):
    grid_pre = jnp.dot(to_grid, pre_flat, preferred_element_type=jnp.float32)
    grid_grad = lax.dot_general(
        from_grid, atom_grad, (((0,), (0,)), ((), ())), preferred_element_type=jnp.float32
    )
    sigmoid_of = jax.nn.sigmoid(grid_pre)
    grid_term = (sigmoid_of * (1.0 + grid_pre * (1.0 - sigmoid_of)) * grid_grad).astype(
        jnp.bfloat16
    )
    return lax.dot_general(
        to_grid, grid_term, (((0,), (0,)), ((), ())), preferred_element_type=jnp.float32
    ).astype(jnp.bfloat16)


def add_parts(right_parts):
    return tuple((right_one for right_one in right_parts))


def per_device_general(
    cotangent,
    wigner,
    sender_ids,
    receiver_slots,
    destinations,
    live_counts,
    receiver_lists,
    weight_zero,
    real_one,
    imag_one,
    real_two,
    imag_two,
    to_grid,
    from_grid,
    pre_act,
):
    edge_total = cotangent.shape[2]
    block_count = destinations.shape[0]
    block_width = edge_total // block_count
    coef_rows = pre_act.shape[0]
    chan_share = pre_act.shape[1]
    atom_share = pre_act.shape[2]
    slot_width = receiver_lists.shape[1]
    shard_count = lax.axis_size("atoms")
    per_dest = (block_count + shard_count - 1) // shard_count
    slot_total = shard_count * per_dest
    weights = (weight_zero, real_one, imag_one, real_two, imag_two)
    weight_cols = tuple((weight for weight in weights))
    grad_parts = add_parts(
        so2_transpose(lax.all_gather(cotangent, ("chan", "sub"), axis=1, tiled=True), weight_cols)
    )
    rotated = rotate_back(grad_parts, wigner)
    live_edge = (
        lax.broadcasted_iota(jnp.int32, (block_count, block_width), 1) < live_counts[:, None]
    )
    live_flat = live_edge.reshape(edge_total)
    atom_axis = jnp.arange(atom_share, dtype=jnp.int32)
    sender_rows = rotated[:, 0].reshape(coef_rows * chan_share, edge_total)
    sender_hot = ((sender_ids[:, None] == atom_axis[None, :]) & live_flat[:, None]).astype(
        jnp.bfloat16
    )
    sender_sum = jnp.dot(sender_rows, sender_hot, preferred_element_type=jnp.float32)
    receiver_rows = rotated[:, 1].reshape(coef_rows * chan_share, block_count, block_width)
    slot_grid = receiver_slots.reshape(block_count, block_width)
    slot_axis = jnp.arange(slot_width, dtype=jnp.int32)
    block_axis = jnp.arange(block_count, dtype=jnp.int32)
    same_dest = destinations[:, None] == destinations[None, :]
    earlier = jnp.sum(same_dest & (block_axis[:, None] > block_axis[None, :]), axis=1)
    placement = destinations * per_dest + earlier
    place_hot = placement[:, None] == jnp.arange(slot_total, dtype=jnp.int32)[None, :]
    slot_hot = ((slot_grid[:, :, None] == slot_axis[None, None, :]) & live_edge[:, :, None]).astype(
        jnp.bfloat16
    )
    block_sums = jnp.einsum(
        "kbw,bwr->bkr", receiver_rows, slot_hot, preferred_element_type=jnp.float32
    ).astype(jnp.bfloat16)
    send_sums = jnp.einsum(
        "bs,bkr->ksr",
        place_hot.astype(jnp.bfloat16),
        block_sums,
        preferred_element_type=jnp.float32,
    ).astype(jnp.bfloat16)
    list_send = (
        jnp.sum(place_hot.astype(jnp.int32)[:, :, None] * (receiver_lists[:, None, :] + 1), axis=0)
        - 1
    )
    list_wire = list_send.astype(jnp.float32).astype(jnp.bfloat16)[None]
    got_sums, got_lists = (
        lax.all_to_all(send_sums, "atoms", split_axis=1, concat_axis=1, tiled=True),
        lax.all_to_all(list_wire, "atoms", split_axis=1, concat_axis=1, tiled=True),
    )
    got_ids = got_lists[0].astype(jnp.float32).astype(jnp.int32).reshape(slot_total * slot_width)
    got_hot = (got_ids[:, None] == atom_axis[None, :]).astype(jnp.bfloat16)
    receiver_sum = jnp.dot(
        got_sums.reshape(coef_rows * chan_share, slot_total * slot_width),
        got_hot,
        preferred_element_type=jnp.float32,
    )
    atom_grad = (
        (sender_sum + receiver_sum).astype(jnp.bfloat16).reshape(coef_rows, chan_share * atom_share)
    )
    result = sphere_backward(
        to_grid, from_grid, pre_act.reshape(coef_rows, chan_share * atom_share), atom_grad
    )
    return result.reshape(coef_rows, chan_share, atom_share)


MESH = pl.DeviceIdType.MESH
F32 = jnp.float32
BF16 = jnp.bfloat16


def dot_last(left, right):
    return lax.dot_general(left, right, (((1,), (1,)), ((), ())), preferred_element_type=F32)


def dot_first(left, right):
    return lax.dot_general(left, right, (((0,), (0,)), ((), ())), preferred_element_type=F32)


def rotate_chunk(grads, wig, rotated, columns):
    offset = 0
    for degree in range(7):
        reach = min(degree, 2)
        starts = {-2: 22 + degree, -1: 12 + degree, 0: degree, 1: 6 + degree, 2: 17 + degree}
        rows = [grads[pl.ds(64 * starts[m], 64), columns] for m in range(-reach, reach + 1)]
        width = 2 * degree + 1
        for p in range(width):
            total = None
            for position, row in enumerate(rows):
                at = offset + position * width + p
                term = wig[at : at + 1, columns] * row
                total = term if total is None else total + term
            total = total.astype(BF16)
            for half in range(4):
                rotated[
                    half // 2, half % 2, degree * degree + p, :, columns
                ] = total[16 * half : 16 * half + 16]
        offset += len(rows) * width


def spread(raw, total, top, left, sign):
    outs, halves, ins, rows, width = raw.shape

    def one(i, carry):
        a, h = lax.div(i, halves), lax.rem(i, halves)
        at = pl.ds(pl.multiple_of(top + i * rows, rows), rows)
        for b in range(ins):
            piece = raw[a, h, b]
            total[at, left + b * width : left + b * width + width] = piece if sign > 0 else -piece
        return carry

    lax.fori_loop(0, outs * halves, one, 0)


def fused_kernel(
    chunks,
    cot,
    wigner_hbm,
    senders,
    slots,
    dests,
    lives,
    lists,
    weight_zero,
    real_one,
    imag_one,
    real_two,
    imag_two,
    grid_to,
    from_grid,
    pre_hbm,
    out,
    gathered,
    wigner,
    raw_zero,
    raw_one,
    raw_two,
    wzero,
    wone,
    wtwo,
    pre,
    grads,
    wig,
    rotated,
    hot_recv,
    hot_send,
    acc_recv,
    acc_send,
    send_to,
    recv_to,
    message,
    arrived,
    slope,
    packed,
    tall,
    flat,
    local_sem,
    out_sem,
    in_sem,
    far_out,
    far_in,
):
    x = lax.axis_index("chan")
    core = lax.axis_index("sub")
    z = lax.axis_index("atoms")
    shards = message.shape[0]
    atoms = acc_send.shape[1]
    me, xpart = 2 * x + core, 2 * (1 - x) + core
    cpart, dpart = 2 * x + 1 - core, 2 * (1 - x) + 1 - core
    to_core, to_chip = {"sub": 1 - core}, {"chan": 1 - x}
    edges = cot.shape[2]
    wide = edges // chunks

    barrier = pltpu.get_barrier_semaphore()
    pl.semaphore_signal(barrier, inc=1, device_id=to_core, device_id_type=MESH)
    pl.semaphore_signal(barrier, inc=1, device_id=to_chip, device_id_type=MESH)
    for step in range(1, shards):
        pl.semaphore_signal(
            barrier, inc=1, device_id={"atoms": lax.rem(z + step, shards)}, device_id_type=MESH
        )
    pl.semaphore_wait(barrier, shards + 1)

    def span(j):
        return pl.ds(pl.multiple_of(j * wide, wide), wide)

    def own_copy(j, kind, target):
        return pltpu.make_async_remote_copy(
            src_ref=cot.at[:, :, span(j)],
            dst_ref=gathered.at[:, me, :, span(j)],
            send_sem=out_sem.at[kind, j],
            recv_sem=in_sem.at[kind, j],
            device_id=target,
            device_id_type=MESH,
        )

    def arrival(j, kind, origin, target):
        return pltpu.make_async_remote_copy(
            src_ref=gathered.at[:, origin, :, span(j)],
            dst_ref=gathered.at[:, origin, :, span(j)],
            send_sem=out_sem.at[kind, j],
            recv_sem=in_sem.at[kind, j],
            device_id=target,
            device_id_type=MESH,
        )

    def start_chunk(j, carry):
        own_copy(j, 1, to_chip).start()
        own_copy(j, 0, to_core).start()
        return carry

    lax.fori_loop(0, chunks, start_chunk, 0)
    loads = [
        (pre_hbm, pre),
        (weight_zero, raw_zero),
        (real_one, raw_one.at[0]),
        (imag_one, raw_one.at[1]),
        (real_two, raw_two.at[0]),
        (imag_two, raw_two.at[1]),
        (wigner_hbm, wigner),
        (cot, gathered.at[:, me]),
    ]
    loads = [
        pltpu.make_async_copy(origin, target, local_sem.at[i])
        for i, (origin, target) in enumerate(loads)
    ]
    for load in loads:
        load.start()

    blocks, block = slots.shape
    listed = jnp.zeros((blocks, block), jnp.int32)
    for slot in range(lists.shape[1]):
        listed = jnp.where(slots[...] == slot, lists[:, slot : slot + 1], listed)
    for b in range(blocks):
        live = lax.broadcasted_iota(jnp.int32, (1, block), 1) < lives[b]
        at = slice(b, b + 1)
        recv_to[at, :] = jnp.where(live, dests[b] * atoms + listed[at], -1)
        send_to[at, :] = jnp.where(live, senders[at, :], -1)
    acc_recv[...] = jnp.zeros_like(acc_recv)
    acc_send[...] = jnp.zeros_like(acc_send)

    loads[0].wait()
    packed[:, 0:atoms] = pre[...].astype(F32)
    packed[:, atoms:128] = jnp.zeros((packed.shape[0], 128 - atoms), F32)
    coefs = grid_to.shape[0]
    for c in range(16):
        pair = [
            packed[pl.ds(16 * half + c, coefs, stride=32), :][:, 0:atoms] for half in range(2)
        ]
        flat[:, 128 * c : 128 * c + 128] = jnp.concatenate(pair, axis=1).astype(BF16)

    def slope_part(i, carry):
        columns = pl.ds(pl.multiple_of(i * 256, 256), 256)
        value = dot_first(grid_to[...], flat[:, columns])
        sig = 1.0 / (1.0 + jnp.exp(-value))
        slope[:, columns] = sig * (1.0 + value * (1.0 - sig))
        return carry

    lax.fori_loop(0, 8, slope_part, 0)
    for load in loads[1:]:
        load.wait()
    spread(raw_zero, wzero, 0, 0, 1)
    for both, total in ((raw_one, wone), (raw_two, wtwo)):
        size = total.shape[0] // 2
        spread(both.at[0], total, 0, 0, 1)
        spread(both.at[1], total, 0, size, 1)
        spread(both.at[1], total, size, 0, -1)
        spread(both.at[0], total, size, size, 1)

    def work(j, carry):
        arrival(j, 1, xpart, to_chip).wait_recv()
        arrival(j, 2, xpart, to_core).start()
        arrival(j, 0, cpart, to_core).wait_recv()
        arrival(j, 2, dpart, to_core).wait_recv()
        piece = gathered[:, :, :, span(j)].reshape(29 * 64, wide)
        grads[0:448] = jnp.dot(wzero[...], piece[0:448], preferred_element_type=F32)
        grads[448:1216] = jnp.dot(wone[...], piece[448:1216], preferred_element_type=F32)
        grads[1216:1856] = jnp.dot(wtwo[...], piece[1216:1856], preferred_element_type=F32)
        wig[...] = wigner[:, span(j)].astype(F32)

        for i in range(wide // block):
            columns = pl.ds(i * block, block)
            rotate_chunk(grads, wig, rotated, columns)
            row = pl.ds(j * (wide // block) + i, 1)
            hot_recv[:, columns] = (
                lax.broadcasted_iota(jnp.int32, (hot_recv.shape[0], block), 0) == recv_to[row, :]
            ).astype(F32).astype(BF16)
            hot_send[:, columns] = (
                lax.broadcasted_iota(jnp.int32, (hot_send.shape[0], block), 0) == send_to[row, :]
            ).astype(F32).astype(BF16)
        height = acc_recv.shape[0]
        acc_recv[...] += dot_last(rotated[1].reshape(height, wide), hot_recv[...])
        acc_send[...] += dot_last(rotated[0].reshape(height, wide), hot_send[...])
        return carry

    lax.fori_loop(0, chunks, work, 0)

    half_rows = acc_recv.shape[0] // 2
    for d in range(shards):
        cut = slice(atoms * d, atoms * d + atoms)
        message[d] = jnp.concatenate(
            [acc_recv[0:half_rows, cut], acc_recv[half_rows:, cut]], axis=1
        ).astype(BF16)

    def far_copy(step):
        return pltpu.make_async_remote_copy(
            src_ref=message.at[lax.rem(z + step, shards)],
            dst_ref=arrived.at[step - 1],
            send_sem=far_out.at[step - 1],
            recv_sem=far_in.at[step - 1],
            device_id={"atoms": lax.rem(z + step, shards)},
            device_id_type=MESH,
        )

    for step in range(1, shards):
        far_copy(step).start()
    total = jnp.concatenate([acc_send[0:half_rows], acc_send[half_rows:]], axis=1)
    total = total + message[z].astype(F32)
    for step in range(1, shards):
        far_copy(step).wait_recv()
        total = total + arrived[step - 1].astype(F32)
    tall[...] = total
    for c in range(16):
        flat[:, 128 * c : 128 * c + 128] = tall[pl.ds(c, coefs, stride=16), :].astype(BF16)
    for i in range(8):
        columns = slice(256 * i, 256 * i + 256)
        term = (slope[:, columns] * dot_first(from_grid[...], flat[:, columns])).astype(BF16)
        result = jnp.dot(grid_to[...], term, preferred_element_type=F32)
        for c in range(2):
            tall[pl.ds(2 * i + c, coefs, stride=16), :] = result[:, 128 * c : 128 * c + 128]
    done = tall[...].astype(BF16).reshape(coefs, 16, 128)
    out[:, 0:16, :] = done[:, :, 0:atoms]
    out[:, 16:32, :] = done[:, :, atoms:128]

    def finish(j, carry):
        own_copy(j, 1, to_chip).wait_send()
        own_copy(j, 0, to_core).wait_send()
        arrival(j, 2, xpart, to_core).wait_send()
        return carry

    lax.fori_loop(0, chunks, finish, 0)
    for step in range(1, shards):
        far_copy(step).wait_send()


def per_device(
    mesh,
    cotangent,
    wigner,
    sender_ids,
    receiver_slots,
    destinations,
    live_counts,
    receiver_lists,
    weight_zero,
    real_one,
    imag_one,
    real_two,
    imag_two,
    to_grid,
    from_grid,
    pre_act,
):
    edges = cotangent.shape[2]
    blocks = destinations.shape[0]
    block = edges // blocks
    coefs, chan_share, atoms = pre_act.shape
    shards = mesh.shape["atoms"]
    fits = (
        mesh.shape["chan"] == 2
        and mesh.shape["sub"] == 2
        and cotangent.shape[1] == 16
        and chan_share == 32
        and atoms == 64
        and block == 128
        and blocks % 2 == 0
        and 1 < shards <= 4
    )
    if not fits:
        return per_device_general(
            cotangent,
            wigner,
            sender_ids,
            receiver_slots,
            destinations,
            live_counts,
            receiver_lists,
            weight_zero,
            real_one,
            imag_one,
            real_two,
            imag_two,
            to_grid,
            from_grid,
            pre_act,
        )

    weights = [
        weight.transpose(0, 1, 3, 2, 4)
        for weight in (weight_zero, real_one, imag_one, real_two, imag_two)
    ]
    chunks = blocks // 2
    wide = 2 * block
    height = coefs * chan_share
    points = to_grid.shape[0]
    vmem = pl.BlockSpec(memory_space=pltpu.VMEM)
    smem = pl.BlockSpec(memory_space=pltpu.SMEM)
    hbm = pl.BlockSpec(memory_space=pltpu.HBM)
    return pl.pallas_call(
        functools.partial(fused_kernel, chunks),
        out_shape=jax.ShapeDtypeStruct(pre_act.shape, BF16),
        in_specs=[hbm, hbm, vmem, vmem, smem, smem, vmem] + [hbm] * 5 + [vmem, vmem, hbm],
        out_specs=vmem,
        scratch_shapes=[
            pltpu.VMEM((29, 4, 16, edges), BF16),
            pltpu.VMEM(wigner.shape, BF16),
            pltpu.VMEM(weights[0].shape, BF16),
            pltpu.VMEM((2,) + weights[1].shape, BF16),
            pltpu.VMEM((2,) + weights[3].shape, BF16),
            pltpu.VMEM((448, 448), BF16),
            pltpu.VMEM((768, 768), BF16),
            pltpu.VMEM((640, 640), BF16),
            pltpu.VMEM((height, atoms), BF16),
            pltpu.VMEM((29 * 64, wide), F32),
            pltpu.VMEM((wigner.shape[0], wide), F32),
            pltpu.VMEM((2, 2, coefs, 16, wide), BF16),
            pltpu.VMEM((shards * atoms, wide), BF16),
            pltpu.VMEM((atoms, wide), BF16),
            pltpu.VMEM((height, shards * atoms), F32),
            pltpu.VMEM((height, atoms), F32),
            pltpu.VMEM((blocks, block), jnp.int32),
            pltpu.VMEM((blocks, block), jnp.int32),
            pltpu.VMEM((shards, height // 2, 2 * atoms), BF16),
            pltpu.VMEM((shards - 1, height // 2, 2 * atoms), BF16),
            pltpu.VMEM((points, chan_share * atoms), F32),
            pltpu.VMEM((height, 128), F32),
            pltpu.VMEM((height // 2, 128), F32),
            pltpu.VMEM((coefs, chan_share * atoms), BF16),
            pltpu.SemaphoreType.DMA((8,)),
            pltpu.SemaphoreType.DMA((3, chunks)),
            pltpu.SemaphoreType.DMA((3, chunks)),
            pltpu.SemaphoreType.DMA((shards - 1,)),
            pltpu.SemaphoreType.DMA((shards - 1,)),
        ],
        compiler_params=pltpu.CompilerParams(
            collective_id=0, has_side_effects=True, vmem_limit_bytes=62 * 2**20
        ),
    )(
        cotangent,
        wigner,
        sender_ids.reshape(blocks, block),
        receiver_slots.reshape(blocks, block),
        destinations,
        live_counts,
        receiver_lists,
        *weights,
        to_grid.T,
        from_grid,
        pre_act.reshape(height, atoms),
    )


def solution(mesh):
    in_specs = (
        P(None, ("chan", "sub"), ("groups", "atoms")),
        P(None, ("groups", "atoms")),
        P(("groups", "atoms")),
        P(("groups", "atoms")),
        P(("groups", "atoms")),
        P(("groups", "atoms")),
        P(("groups", "atoms"), None),
        P(None, None, ("chan", "sub"), None, None),
        P(None, None, ("chan", "sub"), None, None),
        P(None, None, ("chan", "sub"), None, None),
        P(None, None, ("chan", "sub"), None, None),
        P(None, None, ("chan", "sub"), None, None),
        P(),
        P(),
        P(None, ("chan", "sub"), ("groups", "atoms")),
    )
    out_specs = P(None, ("chan", "sub"), ("groups", "atoms"))
    return jax.shard_map(
        functools.partial(per_device, mesh), mesh=mesh, in_specs=in_specs, out_specs=out_specs, check_vma=False
    )
```

```python
import functools

import jax
import jax.numpy as jnp
from jax import lax
from jax.experimental import pallas as pl
from jax.experimental.pallas import tpu as pltpu
from jax.sharding import PartitionSpec as P


def contract(weight, piece):
    return jnp.einsum("ahcbq,bqe->ahce", weight, piece, preferred_element_type=jnp.float32)


def so2_transpose(piece, weights):
    weight_zero, real_one, imag_one, real_two, imag_two = weights
    zero_rows = contract(weight_zero, piece[0:7])
    plus_one = contract(real_one, piece[7:13]) + contract(imag_one, piece[13:19])
    minus_one = contract(real_one, piece[13:19]) - contract(imag_one, piece[7:13])
    plus_two = contract(real_two, piece[19:24]) + contract(imag_two, piece[24:29])
    minus_two = contract(real_two, piece[24:29]) - contract(imag_two, piece[19:24])
    return (zero_rows, plus_one, minus_one, plus_two, minus_two)


def rotate_back(grad_parts, wigner):
    zero_rows, plus_one, minus_one, plus_two, minus_two = grad_parts
    pieces_out = []
    offset = 0
    for degree in range(7):
        m_reach = min(degree, 2)
        edge_rows = []
        if m_reach >= 2:
            edge_rows.append(minus_two[degree - 2])
        if m_reach >= 1:
            edge_rows.append(minus_one[degree - 1])
        edge_rows.append(zero_rows[degree])
        if m_reach >= 1:
            edge_rows.append(plus_one[degree - 1])
        if m_reach >= 2:
            edge_rows.append(plus_two[degree - 2])
        span_width = 2 * degree + 1
        summed = jnp.zeros((span_width,) + edge_rows[0].shape, jnp.float32)
        for position, edge_row in enumerate(edge_rows):
            start_row = offset + position * span_width
            coeffs = wigner[start_row : start_row + span_width].astype(jnp.float32)
            summed = summed + coeffs[:, None, None, :] * edge_row[None]
        offset = offset + len(edge_rows) * span_width
        pieces_out.append(summed.astype(jnp.bfloat16))
    return jnp.concatenate(pieces_out, axis=0)


def sphere_backward(to_grid, from_grid, pre_flat, atom_grad):
    grid_pre = jnp.dot(to_grid, pre_flat, preferred_element_type=jnp.float32)
    grid_grad = lax.dot_general(
        from_grid, atom_grad, (((0,), (0,)), ((), ())), preferred_element_type=jnp.float32
    )
    sigmoid_of = jax.nn.sigmoid(grid_pre)
    grid_term = (sigmoid_of * (1.0 + grid_pre * (1.0 - sigmoid_of)) * grid_grad).astype(
        jnp.bfloat16
    )
    return lax.dot_general(
        to_grid, grid_term, (((0,), (0,)), ((), ())), preferred_element_type=jnp.float32
    ).astype(jnp.bfloat16)


def add_parts(right_parts):
    return tuple((right_one for right_one in right_parts))


def per_device_general(
    cotangent,
    wigner,
    sender_ids,
    receiver_slots,
    destinations,
    live_counts,
    receiver_lists,
    weight_zero,
    real_one,
    imag_one,
    real_two,
    imag_two,
    to_grid,
    from_grid,
    pre_act,
):
    edge_total = cotangent.shape[2]
    block_count = destinations.shape[0]
    block_width = edge_total // block_count
    coef_rows = pre_act.shape[0]
    chan_share = pre_act.shape[1]
    atom_share = pre_act.shape[2]
    slot_width = receiver_lists.shape[1]
    shard_count = lax.axis_size("atoms")
    per_dest = (block_count + shard_count - 1) // shard_count
    slot_total = shard_count * per_dest
    weights = (weight_zero, real_one, imag_one, real_two, imag_two)
    weight_cols = tuple((weight for weight in weights))
    grad_parts = add_parts(
        so2_transpose(lax.all_gather(cotangent, ("chan", "sub"), axis=1, tiled=True), weight_cols)
    )
    rotated = rotate_back(grad_parts, wigner)
    live_edge = (
        lax.broadcasted_iota(jnp.int32, (block_count, block_width), 1) < live_counts[:, None]
    )
    live_flat = live_edge.reshape(edge_total)
    atom_axis = jnp.arange(atom_share, dtype=jnp.int32)
    sender_rows = rotated[:, 0].reshape(coef_rows * chan_share, edge_total)
    sender_hot = ((sender_ids[:, None] == atom_axis[None, :]) & live_flat[:, None]).astype(
        jnp.bfloat16
    )
    sender_sum = jnp.dot(sender_rows, sender_hot, preferred_element_type=jnp.float32)
    receiver_rows = rotated[:, 1].reshape(coef_rows * chan_share, block_count, block_width)
    slot_grid = receiver_slots.reshape(block_count, block_width)
    slot_axis = jnp.arange(slot_width, dtype=jnp.int32)
    block_axis = jnp.arange(block_count, dtype=jnp.int32)
    same_dest = destinations[:, None] == destinations[None, :]
    earlier = jnp.sum(same_dest & (block_axis[:, None] > block_axis[None, :]), axis=1)
    placement = destinations * per_dest + earlier
    place_hot = placement[:, None] == jnp.arange(slot_total, dtype=jnp.int32)[None, :]
    slot_hot = ((slot_grid[:, :, None] == slot_axis[None, None, :]) & live_edge[:, :, None]).astype(
        jnp.bfloat16
    )
    block_sums = jnp.einsum(
        "kbw,bwr->bkr", receiver_rows, slot_hot, preferred_element_type=jnp.float32
    ).astype(jnp.bfloat16)
    send_sums = jnp.einsum(
        "bs,bkr->ksr",
        place_hot.astype(jnp.bfloat16),
        block_sums,
        preferred_element_type=jnp.float32,
    ).astype(jnp.bfloat16)
    list_send = (
        jnp.sum(place_hot.astype(jnp.int32)[:, :, None] * (receiver_lists[:, None, :] + 1), axis=0)
        - 1
    )
    list_wire = list_send.astype(jnp.float32).astype(jnp.bfloat16)[None]
    got_sums, got_lists = (
        lax.all_to_all(send_sums, "atoms", split_axis=1, concat_axis=1, tiled=True),
        lax.all_to_all(list_wire, "atoms", split_axis=1, concat_axis=1, tiled=True),
    )
    got_ids = got_lists[0].astype(jnp.float32).astype(jnp.int32).reshape(slot_total * slot_width)
    got_hot = (got_ids[:, None] == atom_axis[None, :]).astype(jnp.bfloat16)
    receiver_sum = jnp.dot(
        got_sums.reshape(coef_rows * chan_share, slot_total * slot_width),
        got_hot,
        preferred_element_type=jnp.float32,
    )
    atom_grad = (
        (sender_sum + receiver_sum).astype(jnp.bfloat16).reshape(coef_rows, chan_share * atom_share)
    )
    result = sphere_backward(
        to_grid, from_grid, pre_act.reshape(coef_rows, chan_share * atom_share), atom_grad
    )
    return result.reshape(coef_rows, chan_share, atom_share)


MESH = pl.DeviceIdType.MESH
F32 = jnp.float32
BF16 = jnp.bfloat16
PARTS = (range(0, 4), range(4, 5), range(5, 6), range(6, 7))
STEPS = {2: (1,), 3: (1, 2), 4: (2, 1, 3)}


def dot_last(left, right):
    return lax.dot_general(left, right, (((1,), (1,)), ((), ())), preferred_element_type=F32)


def dot_first(left, right):
    return lax.dot_general(left, right, (((0,), (0,)), ((), ())), preferred_element_type=F32)


def rotate_chunk(grads, wig, rotated, columns, degrees=range(7)):
    for degree in degrees:
        reach = min(degree, 2)
        offset = sum((2 * min(k, 2) + 1) * (2 * k + 1) for k in range(degree))
        starts = {-2: 22 + degree, -1: 12 + degree, 0: degree, 1: 6 + degree, 2: 17 + degree}
        rows = [grads[pl.ds(64 * starts[m], 64), columns] for m in range(-reach, reach + 1)]
        width = 2 * degree + 1
        for p in range(width):
            total = None
            for position, row in enumerate(rows):
                at = offset + position * width + p
                term = wig[at : at + 1, columns] * row
                total = term if total is None else total + term
            total = total.astype(BF16)
            for half in range(4):
                rotated[
                    half // 2, half % 2, degree * degree + p, :, columns
                ] = total[16 * half : 16 * half + 16]


def spread(raw, total, top, left, sign):
    outs, halves, ins, rows, width = raw.shape

    def one(i, carry):
        a, h = lax.div(i, halves), lax.rem(i, halves)
        at = pl.ds(pl.multiple_of(top + i * rows, rows), rows)
        for b in range(ins):
            piece = raw[a, h, b]
            total[at, left + b * width : left + b * width + width] = piece if sign > 0 else -piece
        return carry

    lax.fori_loop(0, outs * halves, one, 0)


def fused_kernel(
    chunks,
    cot,
    wigner_hbm,
    senders,
    slots,
    dests,
    lives,
    lists,
    weight_zero,
    real_one,
    imag_one,
    real_two,
    imag_two,
    grid_to,
    from_grid,
    pre_hbm,
    out,
    gathered,
    wigner,
    raw_zero,
    raw_one,
    raw_two,
    wzero,
    wone,
    wtwo,
    pre,
    grads,
    wig,
    rotated,
    hot_recv,
    hot_send,
    acc_recv,
    acc_send,
    send_to,
    recv_to,
    message,
    arrived,
    slope,
    packed,
    tall,
    flat,
    local_sem,
    out_sem,
    in_sem,
    far_out,
    far_in,
):
    x = lax.axis_index("chan")
    core = lax.axis_index("sub")
    z = lax.axis_index("atoms")
    shards = message.shape[0]
    atoms = acc_send.shape[1]
    me, xpart = 2 * x + core, 2 * (1 - x) + core
    cpart, dpart = 2 * x + 1 - core, 2 * (1 - x) + 1 - core
    to_core, to_chip = {"sub": 1 - core}, {"chan": 1 - x}
    edges = cot.shape[2]
    wide = edges // chunks

    barrier = pltpu.get_barrier_semaphore()
    pl.semaphore_signal(barrier, inc=1, device_id=to_core, device_id_type=MESH)
    pl.semaphore_signal(barrier, inc=1, device_id=to_chip, device_id_type=MESH)
    for step in range(1, shards):
        pl.semaphore_signal(
            barrier, inc=1, device_id={"atoms": lax.rem(z + step, shards)}, device_id_type=MESH
        )
    pl.semaphore_wait(barrier, shards + 1)

    def span(j):
        return pl.ds(pl.multiple_of(j * wide, wide), wide)

    def own_copy(j, kind, target):
        return pltpu.make_async_remote_copy(
            src_ref=cot.at[:, :, span(j)],
            dst_ref=gathered.at[:, me, :, span(j)],
            send_sem=out_sem.at[kind, j],
            recv_sem=in_sem.at[kind, j],
            device_id=target,
            device_id_type=MESH,
        )

    def arrival(j, kind, origin, target):
        return pltpu.make_async_remote_copy(
            src_ref=gathered.at[:, origin, :, span(j)],
            dst_ref=gathered.at[:, origin, :, span(j)],
            send_sem=out_sem.at[kind, j],
            recv_sem=in_sem.at[kind, j],
            device_id=target,
            device_id_type=MESH,
        )

    def start_chunk(j, carry):
        own_copy(j, 1, to_chip).start()
        own_copy(j, 0, to_core).start()
        return carry

    lax.fori_loop(0, chunks, start_chunk, 0)
    loads = [
        (pre_hbm, pre),
        (weight_zero, raw_zero),
        (real_one, raw_one.at[0]),
        (imag_one, raw_one.at[1]),
        (real_two, raw_two.at[0]),
        (imag_two, raw_two.at[1]),
        (wigner_hbm, wigner),
        (cot, gathered.at[:, me]),
    ]
    loads = [
        pltpu.make_async_copy(origin, target, local_sem.at[i])
        for i, (origin, target) in enumerate(loads)
    ]
    for load in loads:
        load.start()

    blocks, block = slots.shape
    listed = jnp.zeros((blocks, block), jnp.int32)
    for slot in range(lists.shape[1]):
        listed = jnp.where(slots[...] == slot, lists[:, slot : slot + 1], listed)
    for b in range(blocks):
        live = lax.broadcasted_iota(jnp.int32, (1, block), 1) < lives[b]
        at = slice(b, b + 1)
        recv_to[at, :] = jnp.where(live, dests[b] * atoms + listed[at], -1)
        send_to[at, :] = jnp.where(live, senders[at, :], -1)
    acc_recv[...] = jnp.zeros_like(acc_recv)
    acc_send[...] = jnp.zeros_like(acc_send)

    loads[0].wait()
    packed[:, 0:atoms] = pre[...].astype(F32)
    packed[:, atoms:128] = jnp.zeros((packed.shape[0], 128 - atoms), F32)
    coefs = grid_to.shape[0]
    for c in range(16):
        pair = [
            packed[pl.ds(16 * half + c, coefs, stride=32), :][:, 0:atoms] for half in range(2)
        ]
        flat[:, 128 * c : 128 * c + 128] = jnp.concatenate(pair, axis=1).astype(BF16)

    def slope_part(i, carry):
        columns = pl.ds(pl.multiple_of(i * 256, 256), 256)
        value = dot_first(grid_to[...], flat[:, columns])
        sig = 1.0 / (1.0 + jnp.exp(-value))
        slope[:, columns] = sig * (1.0 + value * (1.0 - sig))
        return carry

    lax.fori_loop(0, 8, slope_part, 0)
    for load in loads[1:]:
        load.wait()
    spread(raw_zero, wzero, 0, 0, 1)
    for both, total in ((raw_one, wone), (raw_two, wtwo)):
        size = total.shape[0] // 2
        spread(both.at[0], total, 0, 0, 1)
        spread(both.at[1], total, 0, size, 1)
        spread(both.at[1], total, size, 0, -1)
        spread(both.at[0], total, size, size, 1)

    half_rows = acc_recv.shape[0] // 2

    def far_copy(step, part):
        first, last = PARTS[part][0] ** 2, PARTS[part][-1] ** 2 + 2 * PARTS[part][-1] + 1
        rows = pl.ds(16 * first, 16 * (last - first))
        return pltpu.make_async_remote_copy(
            src_ref=message.at[lax.rem(z + step, shards), rows],
            dst_ref=arrived.at[step - 1, rows],
            send_sem=far_out.at[step - 1, part],
            recv_sem=far_in.at[step - 1, part],
            device_id={"atoms": lax.rem(z + step, shards)},
            device_id_type=MESH,
        )

    def prepare(j):
        arrival(j, 1, xpart, to_chip).wait_recv()
        arrival(j, 2, xpart, to_core).start()
        wig[...] = wigner[:, span(j)].astype(F32)
        for i in range(wide // block):
            columns = pl.ds(i * block, block)
            row = pl.ds(j * (wide // block) + i, 1)
            hot_recv[:, columns] = (
                lax.broadcasted_iota(jnp.int32, (hot_recv.shape[0], block), 0) == recv_to[row, :]
            ).astype(F32).astype(BF16)
            hot_send[:, columns] = (
                lax.broadcasted_iota(jnp.int32, (hot_send.shape[0], block), 0) == send_to[row, :]
            ).astype(F32).astype(BF16)
        arrival(j, 0, cpart, to_core).wait_recv()
        arrival(j, 2, dpart, to_core).wait_recv()
        piece = gathered[:, :, :, span(j)].reshape(29 * 64, wide)
        grads[0:448] = jnp.dot(wzero[...], piece[0:448], preferred_element_type=F32)
        grads[448:1216] = jnp.dot(wone[...], piece[448:1216], preferred_element_type=F32)
        grads[1216:1856] = jnp.dot(wtwo[...], piece[1216:1856], preferred_element_type=F32)

    def work(j, carry):
        prepare(j)
        for i in range(wide // block):
            rotate_chunk(grads, wig, rotated, pl.ds(i * block, block))
        height = acc_recv.shape[0]
        acc_recv[...] += dot_last(rotated[1].reshape(height, wide), hot_recv[...])
        acc_send[...] += dot_last(rotated[0].reshape(height, wide), hot_send[...])
        return carry

    lax.fori_loop(0, chunks - 1, work, 0)

    prepare(chunks - 1)
    for part, degrees in enumerate(PARTS):
        first, last = degrees[0] ** 2, degrees[-1] ** 2 + 2 * degrees[-1] + 1
        for i in range(wide // block):
            rotate_chunk(grads, wig, rotated, pl.ds(i * block, block), degrees)
        rows = slice(16 * first, 16 * last)

        def finished(h, acc, hot):
            return [
                acc[half * half_rows + 16 * first : half * half_rows + 16 * last, :]
                + dot_last(rotated[h, half, first:last].reshape(16 * (last - first), wide), hot[...])
                for half in range(2)
            ]

        pair = finished(1, acc_recv, hot_recv)
        for d in range(shards):
            cut = slice(atoms * d, atoms * d + atoms)
            message[d, rows] = jnp.concatenate([pair[0][:, cut], pair[1][:, cut]], axis=1).astype(BF16)
        for step in STEPS[shards]:
            far_copy(step, part).start()
        tall[rows] = jnp.concatenate(finished(0, acc_send, hot_send), axis=1)
    for part, degrees in enumerate(PARTS):
        rows = slice(16 * degrees[0] ** 2, 16 * (degrees[-1] ** 2 + 2 * degrees[-1] + 1))
        total = tall[rows] + message[z, rows].astype(F32)
        for step in STEPS[shards]:
            far_copy(step, part).wait_recv()
            total = total + arrived[step - 1, rows].astype(F32)
        tall[rows] = total
    for c in range(16):
        flat[:, 128 * c : 128 * c + 128] = tall[pl.ds(c, coefs, stride=16), :].astype(BF16)
    for i in range(8):
        columns = slice(256 * i, 256 * i + 256)
        term = (slope[:, columns] * dot_first(from_grid[...], flat[:, columns])).astype(BF16)
        result = jnp.dot(grid_to[...], term, preferred_element_type=F32)
        for c in range(2):
            tall[pl.ds(2 * i + c, coefs, stride=16), :] = result[:, 128 * c : 128 * c + 128]
    done = tall[...].astype(BF16).reshape(coefs, 16, 128)
    out[:, 0:16, :] = done[:, :, 0:atoms]
    out[:, 16:32, :] = done[:, :, atoms:128]

    def finish(j, carry):
        own_copy(j, 1, to_chip).wait_send()
        own_copy(j, 0, to_core).wait_send()
        arrival(j, 2, xpart, to_core).wait_send()
        return carry

    lax.fori_loop(0, chunks, finish, 0)
    for part in range(len(PARTS)):
        for step in STEPS[shards]:
            far_copy(step, part).wait_send()


def per_device(
    mesh,
    cotangent,
    wigner,
    sender_ids,
    receiver_slots,
    destinations,
    live_counts,
    receiver_lists,
    weight_zero,
    real_one,
    imag_one,
    real_two,
    imag_two,
    to_grid,
    from_grid,
    pre_act,
):
    edges = cotangent.shape[2]
    blocks = destinations.shape[0]
    block = edges // blocks
    coefs, chan_share, atoms = pre_act.shape
    shards = mesh.shape["atoms"]
    fits = (
        mesh.shape["chan"] == 2
        and mesh.shape["sub"] == 2
        and cotangent.shape[1] == 16
        and chan_share == 32
        and atoms == 64
        and block == 128
        and blocks % 2 == 0
        and 1 < shards <= 4
    )
    if not fits:
        return per_device_general(
            cotangent,
            wigner,
            sender_ids,
            receiver_slots,
            destinations,
            live_counts,
            receiver_lists,
            weight_zero,
            real_one,
            imag_one,
            real_two,
            imag_two,
            to_grid,
            from_grid,
            pre_act,
        )

    weights = [
        weight.transpose(0, 1, 3, 2, 4)
        for weight in (weight_zero, real_one, imag_one, real_two, imag_two)
    ]
    chunks = blocks // 2
    wide = 2 * block
    height = coefs * chan_share
    points = to_grid.shape[0]
    vmem = pl.BlockSpec(memory_space=pltpu.VMEM)
    smem = pl.BlockSpec(memory_space=pltpu.SMEM)
    hbm = pl.BlockSpec(memory_space=pltpu.HBM)
    return pl.pallas_call(
        functools.partial(fused_kernel, chunks),
        out_shape=jax.ShapeDtypeStruct(pre_act.shape, BF16),
        in_specs=[hbm, hbm, vmem, vmem, smem, smem, vmem] + [hbm] * 5 + [vmem, vmem, hbm],
        out_specs=vmem,
        scratch_shapes=[
            pltpu.VMEM((29, 4, 16, edges), BF16),
            pltpu.VMEM(wigner.shape, BF16),
            pltpu.VMEM(weights[0].shape, BF16),
            pltpu.VMEM((2,) + weights[1].shape, BF16),
            pltpu.VMEM((2,) + weights[3].shape, BF16),
            pltpu.VMEM((448, 448), BF16),
            pltpu.VMEM((768, 768), BF16),
            pltpu.VMEM((640, 640), BF16),
            pltpu.VMEM((height, atoms), BF16),
            pltpu.VMEM((29 * 64, wide), F32),
            pltpu.VMEM((wigner.shape[0], wide), F32),
            pltpu.VMEM((2, 2, coefs, 16, wide), BF16),
            pltpu.VMEM((shards * atoms, wide), BF16),
            pltpu.VMEM((atoms, wide), BF16),
            pltpu.VMEM((height, shards * atoms), F32),
            pltpu.VMEM((height, atoms), F32),
            pltpu.VMEM((blocks, block), jnp.int32),
            pltpu.VMEM((blocks, block), jnp.int32),
            pltpu.VMEM((shards, height // 2, 2 * atoms), BF16),
            pltpu.VMEM((shards - 1, height // 2, 2 * atoms), BF16),
            pltpu.VMEM((points, chan_share * atoms), F32),
            pltpu.VMEM((height, 128), F32),
            pltpu.VMEM((height // 2, 128), F32),
            pltpu.VMEM((coefs, chan_share * atoms), BF16),
            pltpu.SemaphoreType.DMA((8,)),
            pltpu.SemaphoreType.DMA((3, chunks)),
            pltpu.SemaphoreType.DMA((3, chunks)),
            pltpu.SemaphoreType.DMA((shards - 1, len(PARTS))),
            pltpu.SemaphoreType.DMA((shards - 1, len(PARTS))),
        ],
        compiler_params=pltpu.CompilerParams(
            collective_id=0, has_side_effects=True, vmem_limit_bytes=62 * 2**20
        ),
    )(
        cotangent,
        wigner,
        sender_ids.reshape(blocks, block),
        receiver_slots.reshape(blocks, block),
        destinations,
        live_counts,
        receiver_lists,
        *weights,
        to_grid.T,
        from_grid,
        pre_act.reshape(height, atoms),
    )


def solution(mesh):
    in_specs = (
        P(None, ("chan", "sub"), ("groups", "atoms")),
        P(None, ("groups", "atoms")),
        P(("groups", "atoms")),
        P(("groups", "atoms")),
        P(("groups", "atoms")),
        P(("groups", "atoms")),
        P(("groups", "atoms"), None),
        P(None, None, ("chan", "sub"), None, None),
        P(None, None, ("chan", "sub"), None, None),
        P(None, None, ("chan", "sub"), None, None),
        P(None, None, ("chan", "sub"), None, None),
        P(None, None, ("chan", "sub"), None, None),
        P(),
        P(),
        P(None, ("chan", "sub"), ("groups", "atoms")),
    )
    out_specs = P(None, ("chan", "sub"), ("groups", "atoms"))
    return jax.shard_map(
        functools.partial(per_device, mesh), mesh=mesh, in_specs=in_specs, out_specs=out_specs, check_vma=False
    )
```
